32 devices in a mesh: grp: 2 (over y), seg: 16 (over z, x, core).
Axes of the slice: x: 2, y: 2, z: 4, core: 2. Of those that a mesh axis runs over, the one named last changes fastest.
Arguments:
- waveform: bfloat16 [512, 256, 512], P('grp', 'seg')
- valid_count: int32 [512, 256], P('grp', 'seg'), may hold values from 128 to 512
- plan: int32 [2, 8], replicated, may hold values from 0 to 1, as said below
Outputs:
- cross: bfloat16 [128, 2, 512, 8, 256], P('seg', None, 'grp')
The draws below stay inside these ranges and needn't reach their ends.
Inputs may be any that keep to these rules, and one draw needn't show every extreme that they name: `plan`: row g lists, round by round, the partner group of group g: in every round g is the partner of its partner and each group is named once, and every row names each of the 2 groups at least once.
All inputs are finite; a program needn't handle non-finite values.
Results may differ from the reference program's by a relative error of at most 0.0061.
Values may be sent and summed in bfloat16 or wider, within the bound.
No kernel may reach another device: no remote copies, remote signals or barrier semaphores. Data moves between devices by JAX's collectives and lax.ppermute only.
A program may use at most 128 MiB of HBM per device.

```python
import math
import jax
import jax.numpy as jnp
from jax import lax

SG = 256
F = 128
SAMPLES = 512
K0 = 2
NGROUPS = 2
ROUNDS = 8
STATIONS = 512
SEGS = 256


def draw_waveform(key, part):
    key = jax.random.fold_in(key, 3)
    key_level, key_noise = jax.random.split(key, 2)
    level = jnp.exp(jax.random.uniform(key_level, (STATIONS, SEGS, 1), minval=0.0, maxval=math.log(10.0)))
    noise = jax.random.normal(key_noise, (STATIONS, SEGS, SAMPLES))
    return (level * noise).astype(jnp.float32).astype(jnp.bfloat16)


def draw_plan(key, part):
    key = jax.random.fold_in(key, 7)
    key_perm, key_more = jax.random.split(key, 2)
    first = jax.random.permutation(key_perm, NGROUPS).astype(jnp.int32)
    extra = jax.random.randint(key_more, (ROUNDS - NGROUPS,), 0, NGROUPS).astype(jnp.int32)
    masks = jnp.concatenate([first, extra], axis=0).astype(jnp.int32)
    groups = jnp.arange(NGROUPS, dtype=jnp.int32)
    return jnp.bitwise_xor(groups[:, None], masks[None, :]).astype(jnp.int32)


def set_ends(array, rng, smallest, top_value):
    extent = array.shape
    spot = [jax.random.randint(jax.random.fold_in(rng, axis), (), 0, extent[axis]) for axis in range(len(extent))]
    array = array.at[tuple(spot)].set(smallest)
    longest = extent.index(max(extent))
    spot[longest] = (spot[longest] + 1) % extent[longest]
    return array.at[tuple(spot)].set(top_value)


def setup_inputs(seed: int = 0) -> dict:
    key_list = jax.random.split(jax.random.key(seed), 4)
    return {
        "waveform": draw_waveform(jax.random.fold_in(key_list[3], 71), 0),
        "valid_count": set_ends(jax.random.randint(key_list[1], (STATIONS, SEGS), SAMPLES // 4, SAMPLES + 1), jax.random.fold_in(key_list[1], 1), SAMPLES // 4, SAMPLES).astype(jnp.int32),
        "plan": draw_plan(jax.random.fold_in(key_list[3], 71), 0),
    }


def make_basis(samples):
    times = jnp.arange(samples, dtype=jnp.int32)[:, None]
    bins = K0 + jnp.arange(F, dtype=jnp.int32)[None, :]
    phase = (times * bins % samples).astype(jnp.float32) * (2.0 * math.pi / samples)
    return jnp.concatenate([jnp.cos(phase), -jnp.sin(phase)], axis=1).astype(jnp.bfloat16)

def reference(waveform, valid_count, plan):
    basis = make_basis(SAMPLES)
    times = jnp.arange(SAMPLES, dtype=jnp.int32)
    gated = jnp.where(times[None, None, :] < valid_count[:, :, None], waveform, jnp.zeros_like(waveform))
    spectrum = jnp.dot(gated.reshape(STATIONS * SEGS, SAMPLES), basis, preferred_element_type=jnp.float32)
    spectrum = spectrum.reshape(STATIONS, SEGS, 2 * F)
    power = lax.optimization_barrier(jnp.sum(spectrum * spectrum, axis=-1)) / F
    keep = (valid_count >= SAMPLES // 2).astype(jnp.float32)
    weight = keep / jnp.sqrt(power + 1e-06)
    white = (spectrum * weight[:, :, None]).astype(jnp.bfloat16)
    owner = jnp.arange(STATIONS, dtype=jnp.int32) // SG
    columns = plan[owner][:, :, None] * SG + jnp.arange(SG, dtype=jnp.int32)[None, None, :]
    station_rows = jnp.arange(STATIONS, dtype=jnp.int32)[:, None, None]

    def one_bin(index):
        real_part = lax.dynamic_index_in_dim(white, index, 2, keepdims=False)
        imag_part = lax.dynamic_index_in_dim(white, index + F, 2, keepdims=False)
        cross_re = jnp.dot(real_part, real_part.T, preferred_element_type=jnp.float32) + jnp.dot(imag_part, imag_part.T, preferred_element_type=jnp.float32)
        cross_im = jnp.dot(imag_part, real_part.T, preferred_element_type=jnp.float32) - jnp.dot(real_part, imag_part.T, preferred_element_type=jnp.float32)
        full = jnp.stack([cross_re, cross_im], axis=0) / SEGS
        picked = full[:, station_rows, columns]
        return picked.astype(jnp.bfloat16)
    return lax.map(one_bin, jnp.arange(F, dtype=jnp.int32))
```

```python
import functools
import math

import jax
import jax.numpy as jnp
import numpy as np
from jax import lax
from jax.experimental import pallas as pl
from jax.experimental.pallas import tpu as pltpu
from jax.sharding import PartitionSpec as P

F = 128
K0 = 2
PLANES = 4
LANES = 128
MIB = 1024 * 1024


def make_basis(samples, parts):
    bins = np.arange(F).reshape(parts, 1, F // parts)
    bins = np.concatenate([bins, bins], axis=1)
    imag = np.zeros_like(bins)
    imag[:, 1] = 1
    bins, imag = bins.reshape(-1, 1), imag.reshape(-1, 1)
    phase = (np.arange(samples)[None, :] * (K0 + bins) % samples) * (2.0 * math.pi / samples)
    return np.where(imag == 1, -np.sin(phase), np.cos(phase))


def head_kernel(me_ref, wave_ref, valid_ref, basis_ref, *rest, parts):
    out_refs, (held_ref, wide_ref, white_ref, sems) = rest[:-4], rest[-4:]
    rows, segs, samples = wave_ref.shape
    half = samples // 2
    step, copies = 16, sems.shape[0]
    share = rows // copies
    sample_tiles, row_tiles = samples // LANES, rows // LANES

    def copy(n):
        part = pl.ds(n * share, share)
        return pltpu.make_async_copy(wave_ref.at[part], held_ref.at[part], sems.at[n])

    for n in range(copies):
        copy(n).start()
    for n in range(copies):
        copy(n).wait()

        @pl.loop(n * share // step, (n + 1) * share // step)
        def _(j):
            block = held_ref[pl.ds(j * step, step)].astype(jnp.float32).reshape(step * segs, samples)
            for q in range(sample_tiles):
                wide_ref[q, pl.ds(pl.multiple_of(j * step * segs, step * segs), step * segs), :] = block[
                    :, q * LANES : (q + 1) * LANES
                ]

    valid_rows = valid_ref[...]
    valid_cols = valid_rows.T
    times = lax.broadcasted_iota(jnp.int32, (rows, LANES), 1)
    for s in range(segs):
        count = valid_cols[:, s : s + 1]
        gated = jnp.concatenate(
            [
                jnp.where(times + q * LANES < count, wide_ref[q, pl.ds(s, rows, stride=segs), :], 0.0)
                for q in range(sample_tiles)
            ],
            axis=1,
        ).astype(jnp.bfloat16)
        spectrum = lax.dot_general(
            basis_ref[...], gated, (((1,), (1,)), ((), ())), preferred_element_type=jnp.float32
        )
        power = jnp.sum(spectrum * spectrum, axis=0, keepdims=True) / F
        keep = (valid_rows[s : s + 1, :] >= half).astype(jnp.float32)
        white = spectrum * (keep / jnp.sqrt(power + 1e-06))
        for q in range(row_tiles):
            white_ref[q, pl.ds(s, 2 * F, stride=segs), :] = white[:, q * LANES : (q + 1) * LANES]

    me = me_ref[0]
    bins_local = F // parts
    span = bins_local * segs

    def put(d, out_ref, index):
        for part in range(2):
            first = pl.multiple_of(((me ^ d) * 2 + part) * span, span)
            piece = jnp.concatenate([white_ref[q, pl.ds(first, span), :] for q in range(row_tiles)], axis=1)
            out_ref[index, part] = piece.astype(jnp.bfloat16).reshape(bins_local, segs, rows)

    for pair, out_ref in enumerate(out_refs[:-1]):
        put(2 * pair, out_ref, 0)
        put(2 * pair + 1, out_refs[-1], pair)


def head(waveform, valid_count, me, parts):
    rows, segs, samples = waveform.shape
    basis = jnp.asarray(make_basis(samples, parts), dtype=jnp.bfloat16)
    vmem = pl.BlockSpec(memory_space=pltpu.VMEM)
    pairs = parts // 2
    block = (2, F // parts, segs, rows)
    return pl.pallas_call(
        functools.partial(head_kernel, parts=parts),
        out_shape=[jax.ShapeDtypeStruct((n,) + block, jnp.bfloat16) for n in [1] * pairs + [pairs]],
        in_specs=[pl.BlockSpec(memory_space=pltpu.SMEM), pl.BlockSpec(memory_space=pltpu.HBM), vmem, vmem],
        out_specs=[vmem] * (pairs + 1),
        scratch_shapes=[
            pltpu.VMEM(waveform.shape, waveform.dtype),
            pltpu.VMEM((samples // LANES, rows * segs, LANES), jnp.float32),
            pltpu.VMEM((rows // LANES, 2 * F * segs, LANES), jnp.float32),
            pltpu.SemaphoreType.DMA((4,)),
        ],
        compiler_params=pltpu.CompilerParams(vmem_limit_bytes=48 * MIB),
        name="spectra",
    )(me[None].astype(jnp.int32), waveform, valid_count.T, basis)


def cross_kernel(select_ref, *rest, groups, held, low):
    pieces = len(held)
    sides = [rest[e * pieces : (e + 1) * pieces] for e in range(groups)]
    out_ref = rest[-1]
    _, _, rows, rounds, columns = out_ref.shape
    chunk = select_ref.shape[0] // rounds
    k = low + pl.program_id(0)

    def whole(e, part):
        return jnp.concatenate(
            [ref[:, part, k - first].reshape(-1, columns) for first, ref in zip(held, sides[e])], axis=0
        )

    real, imag = whole(0, 0), whole(0, 1)
    seg_total = real.shape[0]
    real, imag = real.T, imag.T
    left = jnp.concatenate(
        [jnp.concatenate([real, imag], axis=1), jnp.concatenate([imag, -real], axis=1)], axis=0
    )
    sums = []
    for e in range(groups):
        right = jnp.concatenate([whole(e, 0), whole(e, 1)], axis=0)
        total = jnp.dot(left, right, preferred_element_type=jnp.float32) / float(seg_total)
        sums.append(total.astype(jnp.bfloat16))
    for part in range(2):
        for first in range(0, rows, chunk):
            start = part * rows + first
            values = jnp.concatenate([total[start : start + chunk] for total in sums], axis=0)
            filled = jnp.dot(select_ref[...], values, preferred_element_type=jnp.float32)
            out_ref[0, part, first : first + chunk] = filled.reshape(chunk, rounds, columns).astype(jnp.bfloat16)


def selection(offset, groups, rows):
    chunk = max(16, rows // groups)
    shape = (chunk, offset.shape[0], groups, chunk)
    pick = lax.broadcasted_iota(jnp.int32, shape, 2) == offset[None, :, None, None]
    same = lax.broadcasted_iota(jnp.int32, shape, 0) == lax.broadcasted_iota(jnp.int32, shape, 3)
    return (pick & same).astype(jnp.bfloat16).reshape(chunk * offset.shape[0], groups * chunk)


def add_bins(out, select, sides, held, low, high, bins_local, rounds):
    groups = len(sides)
    segs, rows = sides[0][0].shape[3:]
    seg_total = segs * sum(piece.shape[0] for piece in sides[0])
    pieces = [piece for side in sides for piece in side]
    bins = high - low
    aliased = out is not None
    vmem = pl.BlockSpec(memory_space=pltpu.VMEM)
    return pl.pallas_call(
        functools.partial(cross_kernel, groups=groups, held=held, low=low),
        grid=(bins,),
        out_shape=jax.ShapeDtypeStruct((bins_local, 2, rows, rounds, rows), jnp.bfloat16),
        in_specs=[vmem] * (1 + len(pieces)) + [pl.BlockSpec(memory_space=pl.ANY)] * aliased,
        out_specs=pl.BlockSpec((1, 2, rows, rounds, rows), lambda b: (low + b, 0, 0, 0, 0)),
        input_output_aliases={1 + len(pieces): 0} if aliased else {},
        compiler_params=pltpu.CompilerParams(vmem_limit_bytes=40 * MIB),
        cost_estimate=pl.CostEstimate(
            flops=8 * bins * groups * rows * rows * seg_total,
            bytes_accessed=4 * bins * rows * rounds * rows,
            transcendentals=0,
        ),
        name="cross",
    )(select, *pieces, *([out] if aliased else []))


class Lane:
    def __init__(self, window):
        self.window = window
        self.sent = []

    def send(self, block, axis, pairs, after=()):
        after = list(after) + self.sent[-self.window :][: len(self.sent) // self.window and 1]
        if after:
            block, _ = lax.optimization_barrier((block, after))
        self.sent.append(lax.ppermute(block, axis, pairs))
        return self.sent[-1]


def shards(waveform, valid_count, plan):
    groups = lax.axis_size("grp")
    parts = lax.axis_size("seg")
    chips = parts // PLANES // 2
    bins_local = F // parts
    middle = (5 * bins_local + 4) // 8
    group = lax.axis_index("grp")
    rounds = plan.shape[1]
    offset = lax.dynamic_index_in_dim(plan, group, 0, keepdims=False) ^ group
    select = selection(offset, groups, waveform.shape[0])

    *mine, for_sibling = head(waveform, valid_count, lax.axis_index("seg"), parts)
    theirs = lax.ppermute(for_sibling, "seg", [(s, s ^ 1) for s in range(parts)])
    seg_lane, far_lane, grp_lane = Lane(parts), Lane(2), Lane(2 * (groups - 1))
    sides = [[] for _ in range(groups)]

    def both(n, low=0, high=bins_local):
        return jnp.concatenate([mine[n], theirs[n : n + 1]], axis=0)[:, :, low:high]

    def scatter(lane, n, low=0, high=bins_local, after=()):
        return lane.send(both(n, low, high), "seg", [(s, s ^ (2 * n)) for s in range(parts)], after)

    def forward(blocks):
        block = jnp.concatenate(blocks, axis=0) if len(blocks) > 1 else blocks[0]
        sides[0].append(block)
        for e in range(1, groups):
            sides[e].append(grp_lane.send(block, "grp", [(g, g ^ e) for g in range(groups)]))
        return sides[1][-1]

    own, beside, far, farthest = (range(p * chips, (p + 1) * chips) for p in range(PLANES))
    forward([both(own[0])])
    own_blocks = [scatter(seg_lane, n) for n in own[1:]]
    own_blocks, select = lax.optimization_barrier((own_blocks, select))
    own_done = forward(own_blocks)
    far_blocks = [scatter(far_lane, n, after=own_blocks if n > far[0] else ()) for n in far]
    beside_blocks = [scatter(seg_lane, n, after=far_blocks[:1] if n > beside[0] else ()) for n in beside]
    beside_done = [forward([block]) for block in beside_blocks][-1]
    far_done = [forward([block]) for block in far_blocks]
    waits = {(0, farthest[0]): [own_done], (0, farthest[-1]): [beside_done]}
    waits[middle, farthest[0]] = [far_done[0]]
    for low, high in ((0, middle), (middle, bins_local)):
        for n in farthest:
            forward([scatter(far_lane, n, low, high, waits.get((low, n), ()))])

    out = None
    whole, last = len(sides[0]) - 2 * chips, chips
    for n, (low, high) in enumerate(((0, middle), (middle, bins_local))):
        held = [0] * whole + [low] * last
        chosen = [side[:whole] + side[whole + n * last :][:last] for side in sides]
        out = add_bins(out, select, chosen, held, low, high, bins_local, rounds)
    return out


def solution(mesh):
    return jax.shard_map(
        shards,
        mesh=mesh,
        in_specs=(P("grp", "seg", None), P("grp", "seg"), P()),
        out_specs=P("seg", None, "grp", None, None),
        check_vma=False,
    )
```

```python
import functools
import math

import jax
import jax.numpy as jnp
import numpy as np
from jax import lax
from jax.experimental import pallas as pl
from jax.experimental.pallas import tpu as pltpu
from jax.sharding import PartitionSpec as P

F = 128
LANES = 128
K0 = 2
PLANES = 4
MIB = 1024 * 1024


def make_basis(samples, parts):
    bins = np.arange(F).reshape(parts, 1, F // parts)
    bins = np.concatenate([bins, bins], axis=1)
    imag = np.zeros_like(bins)
    imag[:, 1] = 1
    bins, imag = bins.reshape(-1, 1), imag.reshape(-1, 1)
    phase = (np.arange(samples)[None, :] * (K0 + bins) % samples) * (2.0 * math.pi / samples)
    return np.where(imag == 1, -np.sin(phase), np.cos(phase))


def swap_matrix(outer, inner):
    shape = (inner * outer, inner * outer)
    row, column = (lax.broadcasted_iota(jnp.int32, shape, axis) for axis in range(2))
    source = (row % outer) * inner + row // outer
    return (source == column).astype(jnp.float32).astype(jnp.bfloat16)


def head_kernel(me_ref, wave_ref, valid_ref, basis_ref, *rest, parts):
    out_refs, (held_ref, gated_ref, white_ref, sems) = rest[:-4], rest[-4:]
    rows, segs, samples = wave_ref.shape
    half = samples // 2
    step, copies = 16, sems.shape[0]
    share = rows // copies

    def copy(n):
        part = pl.ds(n * share, share)
        return pltpu.make_async_copy(wave_ref.at[part], held_ref.at[part], sems.at[n])

    for n in range(copies):
        copy(n).start()
    valid_rows = valid_ref[...]
    valid_cols = valid_rows.T
    times = lax.broadcasted_iota(jnp.int32, (step * segs, samples), 1)
    to_segs = swap_matrix(step, segs)
    for first in range(0, rows, step):
        if first % share == 0:
            copy(first // share).wait()
        block = held_ref[first : first + step].reshape(step * segs, samples)
        block = jnp.dot(to_segs, block, preferred_element_type=jnp.float32)
        count = jnp.concatenate([valid_cols[first : first + step, s : s + 1] for s in range(segs)], axis=0)
        block = jnp.where(times < count, block, 0.0).astype(jnp.bfloat16)
        gated_ref[:, first : first + step] = block.reshape(segs, step, samples)

    for s in range(segs):
        spectrum = lax.dot_general(
            basis_ref[...], gated_ref[s], (((1,), (1,)), ((), ())), preferred_element_type=jnp.float32
        )
        power = jnp.sum(spectrum * spectrum, axis=0, keepdims=True) / F
        keep = (valid_rows[s : s + 1, :] >= half).astype(jnp.float32)
        white_ref[s] = spectrum * (keep / jnp.sqrt(power + 1e-06))

    me = me_ref[0]
    span = 2 * F // parts
    to_bins = swap_matrix(segs, span)

    def block_for(d):
        first = pl.multiple_of((me ^ d) * span, span)
        piece = jnp.concatenate([white_ref[s, pl.ds(first, span), :] for s in range(segs)], axis=0)
        piece = jnp.dot(to_bins, piece.astype(jnp.bfloat16), preferred_element_type=jnp.float32)
        return piece.astype(jnp.bfloat16).reshape(2, span // 2, segs, rows)

    for pair, out_ref in enumerate(out_refs[:-1]):
        out_ref[0] = block_for(2 * pair)
        out_refs[-1][pair] = block_for(2 * pair + 1)


def head(waveform, valid_count, me, parts):
    rows, segs, samples = waveform.shape
    basis = jnp.asarray(make_basis(samples, parts), dtype=jnp.bfloat16)
    vmem = pl.BlockSpec(memory_space=pltpu.VMEM)
    pairs = parts // 2
    block = (2, F // parts, segs, rows)
    return pl.pallas_call(
        functools.partial(head_kernel, parts=parts),
        out_shape=[jax.ShapeDtypeStruct((n,) + block, jnp.bfloat16) for n in [1] * pairs + [pairs]],
        in_specs=[pl.BlockSpec(memory_space=pltpu.SMEM), pl.BlockSpec(memory_space=pltpu.HBM), vmem, vmem],
        out_specs=[vmem] * (pairs + 1),
        scratch_shapes=[
            pltpu.VMEM(waveform.shape, waveform.dtype),
            pltpu.VMEM((segs, rows, samples), jnp.bfloat16),
            pltpu.VMEM((segs, 2 * F, rows), jnp.float32),
            pltpu.SemaphoreType.DMA((8,)),
        ],
        compiler_params=pltpu.CompilerParams(vmem_limit_bytes=48 * MIB),
        name="spectra",
    )(me[None].astype(jnp.int32), waveform, valid_count.T, basis)


def cross_kernel(select_ref, *rest, groups, held, low):
    pieces = len(held)
    sides = [rest[e * pieces : (e + 1) * pieces] for e in range(groups)]
    out_ref, held_ref, sems = rest[-3:]
    side_shape = sides[0][0].shape
    rows, columns = side_shape[-1], side_shape[-1]
    rounds, tiles_across = out_ref.shape[2] // (rows * (columns // LANES)), columns // LANES
    chunk = select_ref.shape[0] // rounds
    step, last = pl.program_id(0), pl.num_programs(0) - 1
    slot = step % 2
    k = low + step
    tiles = [(part, first) for part in range(2) for first in range(0, rows, chunk)]

    def copy(n, slot, k):
        part, first = tiles[n]
        height = rounds * tiles_across
        block = pl.ds(first * height, chunk * height)
        return pltpu.make_async_copy(held_ref.at[slot, part, block], out_ref.at[k, part, block], sems.at[slot, n])

    def whole(e, part):
        return jnp.concatenate(
            [ref[:, part, k - first].reshape(-1, columns) for first, ref in zip(held, sides[e])], axis=0
        )

    real, imag = whole(0, 0), whole(0, 1)
    seg_total = real.shape[0]
    real, imag = real.T, imag.T
    left = jnp.concatenate(
        [jnp.concatenate([real, imag], axis=1), jnp.concatenate([imag, -real], axis=1)], axis=0
    )
    sums = []
    for e in range(groups):
        right = jnp.concatenate([whole(e, 0), whole(e, 1)], axis=0)
        total = jnp.dot(left, right, preferred_element_type=jnp.float32) / float(seg_total)
        sums.append(total.astype(jnp.bfloat16))

    @pl.when(step >= 2)
    def _():
        for n in range(len(tiles)):
            copy(n, slot, k - 2).wait()

    for n, (part, first) in enumerate(tiles):
        start = part * rows + first
        values = jnp.concatenate([total[start : start + chunk] for total in sums], axis=0)
        filled = jnp.dot(select_ref[...], values, preferred_element_type=jnp.float32)
        filled = filled.reshape(chunk, rounds, columns)
        filled = jnp.stack([filled[:, :, q * LANES : (q + 1) * LANES] for q in range(tiles_across)], axis=1)
        height = rounds * tiles_across
        held_ref[slot, part, first * height : (first + chunk) * height] = filled.reshape(
            chunk * height, LANES
        ).astype(jnp.bfloat16)
        copy(n, slot, k).start()

    @pl.when(step == last)
    def _():
        for n in range(len(tiles)):
            copy(n, slot, k).wait()

    @pl.when((step == last) & (step > 0))
    def _():
        for n in range(len(tiles)):
            copy(n, 1 - slot, k - 1).wait()


def selection(offset, groups, rows):
    chunk = max(16, rows // groups)
    shape = (chunk, offset.shape[0], groups, chunk)
    pick = lax.broadcasted_iota(jnp.int32, shape, 2) == offset[None, :, None, None]
    same = lax.broadcasted_iota(jnp.int32, shape, 0) == lax.broadcasted_iota(jnp.int32, shape, 3)
    return (pick & same).astype(jnp.bfloat16).reshape(chunk * offset.shape[0], groups * chunk)


def add_bins(out, select, sides, held, low, high, bins_local, rounds):
    groups = len(sides)
    segs, rows = sides[0][0].shape[3:]
    seg_total = segs * sum(piece.shape[0] for piece in sides[0])
    pieces = [piece for side in sides for piece in side]
    bins = high - low
    aliased = out is not None
    vmem = pl.BlockSpec(memory_space=pltpu.VMEM)
    return pl.pallas_call(
        functools.partial(cross_kernel, groups=groups, held=held, low=low),
        grid=(bins,),
        out_shape=jax.ShapeDtypeStruct((bins_local, 2, rows * rounds * (rows // LANES), LANES), jnp.bfloat16),
        in_specs=[vmem] * (1 + len(pieces)) + [pl.BlockSpec(memory_space=pltpu.HBM)] * aliased,
        out_specs=pl.BlockSpec(memory_space=pltpu.HBM),
        scratch_shapes=[
            pltpu.VMEM((2, 2, rows * rounds * (rows // LANES), LANES), jnp.bfloat16),
            pltpu.SemaphoreType.DMA((2, 2 * rows * rounds // select.shape[0])),
        ],
        input_output_aliases={1 + len(pieces): 0} if aliased else {},
        compiler_params=pltpu.CompilerParams(vmem_limit_bytes=40 * MIB),
        cost_estimate=pl.CostEstimate(
            flops=8 * bins * groups * rows * rows * seg_total,
            bytes_accessed=4 * bins * rows * rounds * rows,
            transcendentals=0,
        ),
        name="cross",
    )(select, *pieces, *([out] if aliased else []))


class Lane:
    def __init__(self, window):
        self.window = window
        self.sent = []

    def send(self, block, axis, pairs, after=()):
        after = list(after) + self.sent[-self.window :][: len(self.sent) // self.window and 1]
        if after:
            block, _ = lax.optimization_barrier((block, after))
        self.sent.append(lax.ppermute(block, axis, pairs))
        return self.sent[-1]


def shards(waveform, valid_count, plan):
    groups = lax.axis_size("grp")
    parts = lax.axis_size("seg")
    chips = parts // PLANES // 2
    bins_local = F // parts
    middle = (5 * bins_local + 4) // 8
    group = lax.axis_index("grp")
    rounds = plan.shape[1]
    offset = lax.dynamic_index_in_dim(plan, group, 0, keepdims=False) ^ group
    select = selection(offset, groups, waveform.shape[0])

    *mine, for_sibling = head(waveform, valid_count, lax.axis_index("seg"), parts)
    theirs = lax.ppermute(for_sibling, "seg", [(s, s ^ 1) for s in range(parts)])
    seg_lane, far_lane, grp_lane = Lane(parts), Lane(2), Lane(2 * (groups - 1))
    sides = [[] for _ in range(groups)]

    def both(n, low=0, high=bins_local):
        return jnp.concatenate([mine[n], theirs[n : n + 1]], axis=0)[:, :, low:high]

    def scatter(lane, n, low=0, high=bins_local, after=()):
        return lane.send(both(n, low, high), "seg", [(s, s ^ (2 * n)) for s in range(parts)], after)

    def forward(blocks):
        block = jnp.concatenate(blocks, axis=0) if len(blocks) > 1 else blocks[0]
        sides[0].append(block)
        for e in range(1, groups):
            sides[e].append(grp_lane.send(block, "grp", [(g, g ^ e) for g in range(groups)]))
        return sides[1][-1]

    own, beside, far, farthest = (range(p * chips, (p + 1) * chips) for p in range(PLANES))
    forward([both(own[0])])
    own_blocks = [scatter(seg_lane, n) for n in own[1:]]
    own_blocks, select = lax.optimization_barrier((own_blocks, select))
    own_done = forward(own_blocks)
    far_blocks = [scatter(far_lane, n, after=own_blocks if n > far[0] else ()) for n in far]
    beside_blocks = [scatter(seg_lane, n, after=far_blocks[:1] if n > beside[0] else ()) for n in beside]
    beside_done = [forward([block]) for block in beside_blocks][-1]
    far_done = [forward([block]) for block in far_blocks]
    waits = {(0, farthest[0]): [own_done], (0, farthest[-1]): [beside_done]}
    waits[middle, farthest[0]] = [far_done[0]]
    for low, high in ((0, middle), (middle, bins_local)):
        for n in farthest:
            forward([scatter(far_lane, n, low, high, waits.get((low, n), ()))])

    out = None
    whole, last = len(sides[0]) - 2 * chips, chips
    for n, (low, high) in enumerate(((0, middle), (middle, bins_local))):
        held = [0] * whole + [low] * last
        chosen = [side[:whole] + side[whole + n * last :][:last] for side in sides]
        out = add_bins(out, select, chosen, held, low, high, bins_local, rounds)
    rows = waveform.shape[0]
    out = out.reshape(bins_local, 2, rows, rows // LANES, rounds, LANES).transpose(0, 1, 2, 4, 3, 5)
    return out.reshape(bins_local, 2, rows, rounds, rows)


def solution(mesh):
    return jax.shard_map(
        shards,
        mesh=mesh,
        in_specs=(P("grp", "seg", None), P("grp", "seg"), P()),
        out_specs=P("seg", None, "grp", None, None),
        check_vma=False,
    )
```

```python
import functools
import math

import jax
import jax.numpy as jnp
import numpy as np
from jax import lax
from jax.experimental import pallas as pl
from jax.experimental.pallas import tpu as pltpu
from jax.sharding import PartitionSpec as P

F = 128
LANES = 128
K0 = 2
PLANES = 4
MIB = 1024 * 1024


def make_basis(samples, parts):
    bins = np.arange(F).reshape(parts, 1, F // parts)
    bins = np.concatenate([bins, bins], axis=1)
    imag = np.zeros_like(bins)
    imag[:, 1] = 1
    bins, imag = bins.reshape(-1, 1), imag.reshape(-1, 1)
    phase = (np.arange(samples)[None, :] * (K0 + bins) % samples) * (2.0 * math.pi / samples)
    return np.where(imag == 1, -np.sin(phase), np.cos(phase))


def swap_matrix(outer, inner):
    shape = (inner * outer, inner * outer)
    row, column = (lax.broadcasted_iota(jnp.int32, shape, axis) for axis in range(2))
    source = (row % outer) * inner + row // outer
    return (source == column).astype(jnp.float32).astype(jnp.bfloat16)


def head_kernel(me_ref, wave_ref, valid_ref, basis_ref, *rest, parts):
    out_refs, (held_ref, gated_ref, white_ref, sems) = rest[:-4], rest[-4:]
    rows, segs, samples = wave_ref.shape
    half = samples // 2
    step, copies = 16, sems.shape[0]
    share = rows // copies

    def copy(n):
        part = pl.ds(n * share, share)
        return pltpu.make_async_copy(wave_ref.at[part], held_ref.at[part], sems.at[n])

    for n in range(copies):
        copy(n).start()
    valid_rows = valid_ref[...]
    valid_cols = valid_rows.T
    times = lax.broadcasted_iota(jnp.int32, (step * segs, samples), 1)
    to_segs = swap_matrix(step, segs)
    for first in range(0, rows, step):
        if first % share == 0:
            copy(first // share).wait()
        block = held_ref[first : first + step].reshape(step * segs, samples)
        block = jnp.dot(to_segs, block, preferred_element_type=jnp.float32)
        count = jnp.concatenate([valid_cols[first : first + step, s : s + 1] for s in range(segs)], axis=0)
        block = jnp.where(times < count, block, 0.0).astype(jnp.bfloat16)
        gated_ref[:, first : first + step] = block.reshape(segs, step, samples)

    for s in range(segs):
        spectrum = lax.dot_general(
            basis_ref[...], gated_ref[s], (((1,), (1,)), ((), ())), preferred_element_type=jnp.float32
        )
        power = jnp.sum(spectrum * spectrum, axis=0, keepdims=True) / F
        keep = (valid_rows[s : s + 1, :] >= half).astype(jnp.float32)
        white_ref[s] = spectrum * (keep / jnp.sqrt(power + 1e-06))

    me = me_ref[0]
    span = 2 * F // parts
    to_bins = swap_matrix(segs, span)

    def block_for(d):
        first = pl.multiple_of((me ^ d) * span, span)
        piece = jnp.concatenate([white_ref[s, pl.ds(first, span), :] for s in range(segs)], axis=0)
        piece = jnp.dot(to_bins, piece.astype(jnp.bfloat16), preferred_element_type=jnp.float32)
        return piece.astype(jnp.bfloat16).reshape(2, span // 2, segs, rows)

    for pair, out_ref in enumerate(out_refs[:-1]):
        out_ref[0] = block_for(2 * pair)
        out_refs[-1][pair] = block_for(2 * pair + 1)


def head(waveform, valid_count, me, parts):
    rows, segs, samples = waveform.shape
    basis = jnp.asarray(make_basis(samples, parts), dtype=jnp.bfloat16)
    vmem = pl.BlockSpec(memory_space=pltpu.VMEM)
    pairs = parts // 2
    block = (2, F // parts, segs, rows)
    return pl.pallas_call(
        functools.partial(head_kernel, parts=parts),
        out_shape=[jax.ShapeDtypeStruct((n,) + block, jnp.bfloat16) for n in [1] * pairs + [pairs]],
        in_specs=[pl.BlockSpec(memory_space=pltpu.SMEM), pl.BlockSpec(memory_space=pltpu.HBM), vmem, vmem],
        out_specs=[vmem] * (pairs + 1),
        scratch_shapes=[
            pltpu.VMEM(waveform.shape, waveform.dtype),
            pltpu.VMEM((segs, rows, samples), jnp.bfloat16),
            pltpu.VMEM((segs, 2 * F, rows), jnp.float32),
            pltpu.SemaphoreType.DMA((8,)),
        ],
        compiler_params=pltpu.CompilerParams(vmem_limit_bytes=48 * MIB),
        name="spectra",
    )(me[None].astype(jnp.int32), waveform, valid_count.T, basis)


def cross_kernel(select_ref, *rest, groups, held, low):
    pieces = len(held)
    sides = [rest[e * pieces : (e + 1) * pieces] for e in range(groups)]
    out_ref, held_ref, sems = rest[-3:]
    side_shape = sides[0][0].shape
    rows, columns = side_shape[-1], side_shape[-1]
    rounds, tiles_across = out_ref.shape[2] // (rows * (columns // LANES)), columns // LANES
    chunk = select_ref.shape[0] // rounds
    step, last = pl.program_id(0), pl.num_programs(0) - 1
    slot = step % 2
    k = low + step
    tiles = [(part, first) for part in range(2) for first in range(0, rows, chunk)]

    def copy(n, slot, k):
        part, first = tiles[n]
        height = rounds * tiles_across
        block = pl.ds(first * height, chunk * height)
        return pltpu.make_async_copy(held_ref.at[slot, part, block], out_ref.at[k, part, block], sems.at[slot, n])

    def whole(e, part):
        return jnp.concatenate(
            [ref[:, part, k - first].reshape(-1, columns) for first, ref in zip(held, sides[e])], axis=0
        )

    real, imag = whole(0, 0), whole(0, 1)
    seg_total = real.shape[0]
    real, imag = real.T, imag.T
    left = jnp.concatenate(
        [jnp.concatenate([real, imag], axis=1), jnp.concatenate([imag, -real], axis=1)], axis=0
    )
    sums = []
    for e in range(groups):
        right = jnp.concatenate([whole(e, 0), whole(e, 1)], axis=0)
        total = jnp.dot(left, right, preferred_element_type=jnp.float32) / float(seg_total)
        sums.append(total.astype(jnp.bfloat16))

    @pl.when(step >= 2)
    def _():
        for n in range(len(tiles)):
            copy(n, slot, k - 2).wait()

    for n, (part, first) in enumerate(tiles):
        start = part * rows + first
        values = jnp.concatenate([total[start : start + chunk] for total in sums], axis=0)
        filled = jnp.dot(select_ref[...], values, preferred_element_type=jnp.float32)
        filled = filled.reshape(chunk, rounds, columns)
        filled = jnp.stack([filled[:, :, q * LANES : (q + 1) * LANES] for q in range(tiles_across)], axis=1)
        height = rounds * tiles_across
        held_ref[slot, part, first * height : (first + chunk) * height] = filled.reshape(
            chunk * height, LANES
        ).astype(jnp.bfloat16)
        copy(n, slot, k).start()

    @pl.when(step == last)
    def _():
        for n in range(len(tiles)):
            copy(n, slot, k).wait()

    @pl.when((step == last) & (step > 0))
    def _():
        for n in range(len(tiles)):
            copy(n, 1 - slot, k - 1).wait()


def selection(offset, groups, rows):
    chunk = max(16, rows // groups)
    shape = (chunk, offset.shape[0], groups, chunk)
    pick = lax.broadcasted_iota(jnp.int32, shape, 2) == offset[None, :, None, None]
    same = lax.broadcasted_iota(jnp.int32, shape, 0) == lax.broadcasted_iota(jnp.int32, shape, 3)
    return (pick & same).astype(jnp.bfloat16).reshape(chunk * offset.shape[0], groups * chunk)


def add_bins(out, select, sides, held, low, high, bins_local, rounds):
    groups = len(sides)
    segs, rows = sides[0][0].shape[3:]
    seg_total = segs * sum(piece.shape[0] for piece in sides[0])
    pieces = [piece for side in sides for piece in side]
    bins = high - low
    aliased = out is not None
    vmem = pl.BlockSpec(memory_space=pltpu.VMEM)
    return pl.pallas_call(
        functools.partial(cross_kernel, groups=groups, held=held, low=low),
        grid=(bins,),
        out_shape=jax.ShapeDtypeStruct((bins_local, 2, rows * rounds * (rows // LANES), LANES), jnp.bfloat16),
        in_specs=[vmem] * (1 + len(pieces)) + [pl.BlockSpec(memory_space=pltpu.HBM)] * aliased,
        out_specs=pl.BlockSpec(memory_space=pltpu.HBM),
        scratch_shapes=[
            pltpu.VMEM((2, 2, rows * rounds * (rows // LANES), LANES), jnp.bfloat16),
            pltpu.SemaphoreType.DMA((2, 2 * rows * rounds // select.shape[0])),
        ],
        input_output_aliases={1 + len(pieces): 0} if aliased else {},
        compiler_params=pltpu.CompilerParams(vmem_limit_bytes=40 * MIB),
        cost_estimate=pl.CostEstimate(
            flops=8 * bins * groups * rows * rows * seg_total,
            bytes_accessed=4 * bins * rows * rounds * rows,
            transcendentals=0,
        ),
        name="cross",
    )(select, *pieces, *([out] if aliased else []))


class Lane:
    def __init__(self, window):
        self.window = window
        self.sent = []

    def send(self, block, axis, pairs, after=()):
        after = list(after) + self.sent[-self.window :][: len(self.sent) // self.window and 1]
        if after:
            block, _ = lax.optimization_barrier((block, after))
        self.sent.append(lax.ppermute(block, axis, pairs))
        return self.sent[-1]


def shards(waveform, valid_count, plan):
    groups = lax.axis_size("grp")
    parts = lax.axis_size("seg")
    chips = parts // PLANES // 2
    bins_local = F // parts
    middle = (5 * bins_local + 4) // 8
    group = lax.axis_index("grp")
    rounds = plan.shape[1]
    offset = lax.dynamic_index_in_dim(plan, group, 0, keepdims=False) ^ group
    select = selection(offset, groups, waveform.shape[0])

    *mine, for_sibling = head(waveform, valid_count, lax.axis_index("seg"), parts)
    theirs = lax.ppermute(for_sibling, "seg", [(s, s ^ 1) for s in range(parts)])
    seg_lane, far_lane, grp_lane = Lane(parts), Lane(2), Lane(2 * (groups - 1))
    sides = [[] for _ in range(groups)]

    def both(n, low=0, high=bins_local):
        return jnp.concatenate([mine[n], theirs[n : n + 1]], axis=0)[:, :, low:high]

    def scatter(lane, n, low=0, high=bins_local, after=()):
        return lane.send(both(n, low, high), "seg", [(s, s ^ (2 * n)) for s in range(parts)], after)

    def forward(blocks):
        block = jnp.concatenate(blocks, axis=0) if len(blocks) > 1 else blocks[0]
        sides[0].append(block)
        for e in range(1, groups):
            sides[e].append(grp_lane.send(block, "grp", [(g, g ^ e) for g in range(groups)]))
        return sides[1][-1]

    own, beside, far, farthest = (range(p * chips, (p + 1) * chips) for p in range(PLANES))
    forward([both(own[0])])
    own_blocks = [scatter(seg_lane, n) for n in own[1:]]
    own_blocks, select = lax.optimization_barrier((own_blocks, select))
    own_done = forward(own_blocks)
    waits = {(0, n): own_blocks for n in far[1:]}
    first = [scatter(far_lane, n, 0, middle, waits.get((0, n), ())) for n in far]
    beside_blocks = [scatter(seg_lane, n, after=first[:1] if n > beside[0] else ()) for n in beside]
    beside_done = [forward([block]) for block in beside_blocks]
    far_done = forward(first)
    first = [scatter(far_lane, n, 0, middle, beside_done[:1] if n == farthest[-1] else ()) for n in farthest]
    last_done = [forward([block]) for block in first]
    second = [scatter(far_lane, far[0], middle, bins_local, beside_done[-1:])]
    second += [scatter(far_lane, n, middle, bins_local, [far_done]) for n in far[1:]]
    forward(second)
    split = 1 + chips
    whole = len(sides[0]) - 1 - split
    out = add_bins(
        None, select, [side[: whole + split] for side in sides], [0] * (whole + split), 0, middle, bins_local, rounds
    )
    second = [scatter(far_lane, n, middle, bins_local, last_done[:1]) for n in farthest]
    second[0], out = lax.optimization_barrier((second[0], out))
    for block in second:
        forward([block])
    chosen = [side[:whole] + side[-split:] for side in sides]
    out = add_bins(out, select, chosen, [0] * whole + [middle] * split, middle, bins_local, bins_local, rounds)
    rows = waveform.shape[0]
    out = out.reshape(bins_local, 2, rows, rows // LANES, rounds, LANES).transpose(0, 1, 2, 4, 3, 5)
    return out.reshape(bins_local, 2, rows, rounds, rows)


def solution(mesh):
    return jax.shard_map(
        shards,
        mesh=mesh,
        in_specs=(P("grp", "seg", None), P("grp", "seg"), P()),
        out_specs=P("seg", None, "grp", None, None),
        check_vma=False,
    )
```

```python
import functools
import math

import jax
import jax.numpy as jnp
import numpy as np
from jax import lax
from jax.experimental import pallas as pl
from jax.experimental.pallas import tpu as pltpu
from jax.sharding import PartitionSpec as P

F = 128
LANES = 128
K0 = 2
PLANES = 4
MIB = 1024 * 1024


def make_basis(samples, parts):
    bins = np.arange(F).reshape(parts, 1, F // parts)
    bins = np.concatenate([bins, bins], axis=1)
    imag = np.zeros_like(bins)
    imag[:, 1] = 1
    bins, imag = bins.reshape(-1, 1), imag.reshape(-1, 1)
    phase = (np.arange(samples)[None, :] * (K0 + bins) % samples) * (2.0 * math.pi / samples)
    return np.where(imag == 1, -np.sin(phase), np.cos(phase))


def swap_matrix(outer, inner):
    shape = (inner * outer, inner * outer)
    row, column = (lax.broadcasted_iota(jnp.int32, shape, axis) for axis in range(2))
    source = (row % outer) * inner + row // outer
    return (source == column).astype(jnp.float32).astype(jnp.bfloat16)


def head_kernel(me_ref, wave_ref, valid_ref, basis_ref, *rest, parts):
    out_refs, (held_ref, gated_ref, white_ref, sems) = rest[:-4], rest[-4:]
    rows, segs, samples = wave_ref.shape
    half = samples // 2
    step, copies = 16, sems.shape[0]
    share = rows // copies

    def copy(n):
        part = pl.ds(n * share, share)
        return pltpu.make_async_copy(wave_ref.at[part], held_ref.at[part], sems.at[n])

    for n in range(copies):
        copy(n).start()
    valid_rows = valid_ref[...]
    valid_cols = valid_rows.T
    times = lax.broadcasted_iota(jnp.int32, (step * segs, samples), 1)
    to_segs = swap_matrix(step, segs)
    for first in range(0, rows, step):
        if first % share == 0:
            copy(first // share).wait()
        block = held_ref[first : first + step].reshape(step * segs, samples)
        block = jnp.dot(to_segs, block, preferred_element_type=jnp.float32)
        count = jnp.concatenate([valid_cols[first : first + step, s : s + 1] for s in range(segs)], axis=0)
        block = jnp.where(times < count, block, 0.0).astype(jnp.bfloat16)
        gated_ref[:, first : first + step] = block.reshape(segs, step, samples)

    for s in range(segs):
        spectrum = lax.dot_general(
            basis_ref[...], gated_ref[s], (((1,), (1,)), ((), ())), preferred_element_type=jnp.float32
        )
        power = jnp.sum(spectrum * spectrum, axis=0, keepdims=True) / F
        keep = (valid_rows[s : s + 1, :] >= half).astype(jnp.float32)
        white_ref[s] = spectrum * (keep / jnp.sqrt(power + 1e-06))

    me = me_ref[0]
    span = 2 * F // parts
    to_bins = swap_matrix(segs, span)

    def block_for(d):
        first = pl.multiple_of((me ^ d) * span, span)
        piece = jnp.concatenate([white_ref[s, pl.ds(first, span), :] for s in range(segs)], axis=0)
        piece = jnp.dot(to_bins, piece.astype(jnp.bfloat16), preferred_element_type=jnp.float32)
        return piece.astype(jnp.bfloat16).reshape(2, span // 2, segs, rows)

    for pair, out_ref in enumerate(out_refs[:-1]):
        out_ref[0] = block_for(2 * pair)
        out_refs[-1][pair] = block_for(2 * pair + 1)


def head(waveform, valid_count, me, parts):
    rows, segs, samples = waveform.shape
    basis = jnp.asarray(make_basis(samples, parts), dtype=jnp.bfloat16)
    vmem = pl.BlockSpec(memory_space=pltpu.VMEM)
    pairs = parts // 2
    block = (2, F // parts, segs, rows)
    return pl.pallas_call(
        functools.partial(head_kernel, parts=parts),
        out_shape=[jax.ShapeDtypeStruct((n,) + block, jnp.bfloat16) for n in [1] * pairs + [pairs]],
        in_specs=[pl.BlockSpec(memory_space=pltpu.SMEM), pl.BlockSpec(memory_space=pltpu.HBM), vmem, vmem],
        out_specs=[vmem] * (pairs + 1),
        scratch_shapes=[
            pltpu.VMEM(waveform.shape, waveform.dtype),
            pltpu.VMEM((segs, rows, samples), jnp.bfloat16),
            pltpu.VMEM((segs, 2 * F, rows), jnp.float32),
            pltpu.SemaphoreType.DMA((8,)),
        ],
        compiler_params=pltpu.CompilerParams(vmem_limit_bytes=48 * MIB),
        name="spectra",
    )(me[None].astype(jnp.int32), waveform, valid_count.T, basis)


def cross_kernel(select_ref, *rest, groups, held, low):
    pieces = len(held)
    sides = [rest[e * pieces : (e + 1) * pieces] for e in range(groups)]
    out_ref, held_ref, sems = rest[-3:]
    side_shape = sides[0][0].shape
    rows, columns = side_shape[-1], side_shape[-1]
    rounds, tiles_across = out_ref.shape[2] // (rows * (columns // LANES)), columns // LANES
    chunk = select_ref.shape[0] // rounds
    step, last = pl.program_id(0), pl.num_programs(0) - 1
    slot = step % 2
    k = low + step
    tiles = [(part, first) for part in range(2) for first in range(0, rows, chunk)]

    def copy(n, slot, k):
        part, first = tiles[n]
        height = rounds * tiles_across
        block = pl.ds(first * height, chunk * height)
        return pltpu.make_async_copy(held_ref.at[slot, part, block], out_ref.at[k, part, block], sems.at[slot, n])

    def whole(e, part):
        return jnp.concatenate(
            [ref[:, part, k - first].reshape(-1, columns) for first, ref in zip(held, sides[e])], axis=0
        )

    real, imag = whole(0, 0), whole(0, 1)
    seg_total = real.shape[0]
    real, imag = real.T, imag.T
    left = jnp.concatenate(
        [jnp.concatenate([real, imag], axis=1), jnp.concatenate([imag, -real], axis=1)], axis=0
    )
    sums = []
    for e in range(groups):
        right = jnp.concatenate([whole(e, 0), whole(e, 1)], axis=0)
        total = jnp.dot(left, right, preferred_element_type=jnp.float32) / float(seg_total)
        sums.append(total.astype(jnp.bfloat16))

    @pl.when(step >= 2)
    def _():
        for n in range(len(tiles)):
            copy(n, slot, k - 2).wait()

    for n, (part, first) in enumerate(tiles):
        start = part * rows + first
        values = jnp.concatenate([total[start : start + chunk] for total in sums], axis=0)
        filled = jnp.dot(select_ref[...], values, preferred_element_type=jnp.float32)
        filled = filled.reshape(chunk, rounds, columns)
        filled = jnp.stack([filled[:, :, q * LANES : (q + 1) * LANES] for q in range(tiles_across)], axis=1)
        height = rounds * tiles_across
        held_ref[slot, part, first * height : (first + chunk) * height] = filled.reshape(
            chunk * height, LANES
        ).astype(jnp.bfloat16)
        copy(n, slot, k).start()

    @pl.when(step == last)
    def _():
        for n in range(len(tiles)):
            copy(n, slot, k).wait()

    @pl.when((step == last) & (step > 0))
    def _():
        for n in range(len(tiles)):
            copy(n, 1 - slot, k - 1).wait()


def selection(offset, groups, rows):
    chunk = max(16, rows // groups)
    shape = (chunk, offset.shape[0], groups, chunk)
    pick = lax.broadcasted_iota(jnp.int32, shape, 2) == offset[None, :, None, None]
    same = lax.broadcasted_iota(jnp.int32, shape, 0) == lax.broadcasted_iota(jnp.int32, shape, 3)
    return (pick & same).astype(jnp.bfloat16).reshape(chunk * offset.shape[0], groups * chunk)


def add_bins(out, select, sides, held, low, high, bins_local, rounds):
    groups = len(sides)
    segs, rows = sides[0][0].shape[3:]
    seg_total = segs * sum(piece.shape[0] for piece in sides[0])
    pieces = [piece for side in sides for piece in side]
    bins = high - low
    aliased = out is not None
    vmem = pl.BlockSpec(memory_space=pltpu.VMEM)
    return pl.pallas_call(
        functools.partial(cross_kernel, groups=groups, held=held, low=low),
        grid=(bins,),
        out_shape=jax.ShapeDtypeStruct((bins_local, 2, rows * rounds * (rows // LANES), LANES), jnp.bfloat16),
        in_specs=[vmem] * (1 + len(pieces)) + [pl.BlockSpec(memory_space=pltpu.HBM)] * aliased,
        out_specs=pl.BlockSpec(memory_space=pltpu.HBM),
        scratch_shapes=[
            pltpu.VMEM((2, 2, rows * rounds * (rows // LANES), LANES), jnp.bfloat16),
            pltpu.SemaphoreType.DMA((2, 2 * rows * rounds // select.shape[0])),
        ],
        input_output_aliases={1 + len(pieces): 0} if aliased else {},
        compiler_params=pltpu.CompilerParams(vmem_limit_bytes=40 * MIB),
        cost_estimate=pl.CostEstimate(
            flops=8 * bins * groups * rows * rows * seg_total,
            bytes_accessed=4 * bins * rows * rounds * rows,
            transcendentals=0,
        ),
        name="cross",
    )(select, *pieces, *([out] if aliased else []))


class Lane:
    def __init__(self, window):
        self.window = window
        self.sent = []

    def send(self, block, axis, pairs, after=()):
        after = list(after) + self.sent[-self.window :][: len(self.sent) // self.window and 1]
        if after:
            block, _ = lax.optimization_barrier((block, after))
        self.sent.append(lax.ppermute(block, axis, pairs))
        return self.sent[-1]


def shards(waveform, valid_count, plan):
    groups = lax.axis_size("grp")
    parts = lax.axis_size("seg")
    chips = parts // PLANES // 2
    bins_local = F // parts
    middle = (5 * bins_local + 4) // 8
    halfway = max(1, middle // 2)
    group = lax.axis_index("grp")
    rounds = plan.shape[1]
    offset = lax.dynamic_index_in_dim(plan, group, 0, keepdims=False) ^ group
    select = selection(offset, groups, waveform.shape[0])

    *mine, for_sibling = head(waveform, valid_count, lax.axis_index("seg"), parts)
    theirs = lax.ppermute(for_sibling, "seg", [(s, s ^ 1) for s in range(parts)])
    seg_lane, far_lane, late_lane, grp_lane = Lane(parts), Lane(2), Lane(parts), Lane(3 * (groups - 1))
    sides = [[] for _ in range(groups)]

    def both(n, low=0, high=bins_local):
        return jnp.concatenate([mine[n], theirs[n : n + 1]], axis=0)[:, :, low:high]

    def scatter(lane, n, low=0, high=bins_local, after=()):
        return lane.send(both(n, low, high), "seg", [(s, s ^ (2 * n)) for s in range(parts)], after)

    def forward(blocks):
        block = jnp.concatenate(blocks, axis=0) if len(blocks) > 1 else blocks[0]
        sides[0].append(block)
        for e in range(1, groups):
            sides[e].append(grp_lane.send(block, "grp", [(g, g ^ e) for g in range(groups)]))
        return sides[1][-1]

    own, beside, far, farthest = (range(p * chips, (p + 1) * chips) for p in range(PLANES))
    forward([both(own[0])])
    own_blocks = [scatter(seg_lane, n) for n in own[1:]]
    own_blocks, select = lax.optimization_barrier((own_blocks, select))
    own_done = forward(own_blocks)
    waits = {(0, n): own_blocks for n in far[1:]}
    first = [scatter(far_lane, n, 0, middle, waits.get((0, n), ())) for n in far]
    beside_blocks = [scatter(seg_lane, n, after=own_blocks if n > beside[0] else ()) for n in beside]
    beside_done = [forward([block]) for block in beside_blocks]
    far_done = forward(first)
    first = [scatter(far_lane, n, 0, middle, beside_done[:1] if n == farthest[-1] else ()) for n in farthest]
    last_done = [forward([block]) for block in first]
    second = [scatter(late_lane, far[0], middle, bins_local, [first[0], beside_done[-1]])]
    second += [scatter(late_lane, n, middle, bins_local, [first[-1], far_done]) for n in far[1:]]
    second += [scatter(late_lane, n, middle, bins_local, [first[-1], far_done]) for n in farthest]
    split = 1 + chips
    whole = len(sides[0]) - split
    early = [side[: whole + split] for side in sides]
    out = add_bins(None, select, early, [0] * (whole + split), 0, halfway, bins_local, rounds)
    second, out = lax.optimization_barrier((second, out))
    forward(second[:chips])
    forward(second[chips:])
    out = add_bins(out, select, early, [0] * (whole + split), halfway, middle, bins_local, rounds)
    chosen = [side[:whole] + side[-2:] for side in sides]
    out = add_bins(out, select, chosen, [0] * whole + [middle] * 2, middle, bins_local, bins_local, rounds)
    rows = waveform.shape[0]
    out = out.reshape(bins_local, 2, rows, rows // LANES, rounds, LANES).transpose(0, 1, 2, 4, 3, 5)
    return out.reshape(bins_local, 2, rows, rounds, rows)


def solution(mesh):
    return jax.shard_map(
        shards,
        mesh=mesh,
        in_specs=(P("grp", "seg", None), P("grp", "seg"), P()),
        out_specs=P("seg", None, "grp", None, None),
        check_vma=False,
    )
```

```python
import functools
import math

import jax
import jax.numpy as jnp
import numpy as np
from jax import lax
from jax.experimental import pallas as pl
from jax.experimental.pallas import tpu as pltpu
from jax.sharding import PartitionSpec as P

F = 128
LANES = 128
K0 = 2
PLANES = 4
MIB = 1024 * 1024


def make_basis(samples, parts):
    bins = np.arange(F).reshape(parts, 1, F // parts)
    bins = np.concatenate([bins, bins], axis=1)
    imag = np.zeros_like(bins)
    imag[:, 1] = 1
    bins, imag = bins.reshape(-1, 1), imag.reshape(-1, 1)
    phase = (np.arange(samples)[None, :] * (K0 + bins) % samples) * (2.0 * math.pi / samples)
    return np.where(imag == 1, -np.sin(phase), np.cos(phase))


def swap_matrix(outer, inner):
    shape = (inner * outer, inner * outer)
    row, column = (lax.broadcasted_iota(jnp.int32, shape, axis) for axis in range(2))
    source = (row % outer) * inner + row // outer
    return (source == column).astype(jnp.float32).astype(jnp.bfloat16)


def head_kernel(me_ref, wave_ref, valid_ref, basis_ref, *rest, parts):
    out_refs, (held_ref, gated_ref, white_ref, sems) = rest[:-4], rest[-4:]
    rows, segs, samples = wave_ref.shape
    half = samples // 2
    step, copies = 16, sems.shape[0]
    share = rows // copies

    def copy(n):
        part = pl.ds(n * share, share)
        return pltpu.make_async_copy(wave_ref.at[part], held_ref.at[part], sems.at[n])

    for n in range(copies):
        copy(n).start()
    valid_rows = valid_ref[...]
    valid_cols = valid_rows.T
    times = lax.broadcasted_iota(jnp.int32, (step * segs, samples), 1)
    to_segs = swap_matrix(step, segs)
    for first in range(0, rows, step):
        if first % share == 0:
            copy(first // share).wait()
        block = held_ref[first : first + step].reshape(step * segs, samples)
        block = jnp.dot(to_segs, block, preferred_element_type=jnp.float32)
        count = jnp.concatenate([valid_cols[first : first + step, s : s + 1] for s in range(segs)], axis=0)
        block = jnp.where(times < count, block, 0.0).astype(jnp.bfloat16)
        gated_ref[:, first : first + step] = block.reshape(segs, step, samples)

    for s in range(segs):
        spectrum = lax.dot_general(
            basis_ref[...], gated_ref[s], (((1,), (1,)), ((), ())), preferred_element_type=jnp.float32
        )
        power = jnp.sum(spectrum * spectrum, axis=0, keepdims=True) / F
        keep = (valid_rows[s : s + 1, :] >= half).astype(jnp.float32)
        white_ref[s] = spectrum * (keep / jnp.sqrt(power + 1e-06))

    me = me_ref[0]
    span = 2 * F // parts
    to_bins = swap_matrix(segs, span)

    def block_for(d):
        first = pl.multiple_of((me ^ d) * span, span)
        piece = jnp.concatenate([white_ref[s, pl.ds(first, span), :] for s in range(segs)], axis=0)
        piece = jnp.dot(to_bins, piece.astype(jnp.bfloat16), preferred_element_type=jnp.float32)
        return piece.astype(jnp.bfloat16).reshape(2, span // 2, segs, rows)

    for pair, out_ref in enumerate(out_refs[:-1]):
        out_ref[0] = block_for(2 * pair)
        out_refs[-1][pair] = block_for(2 * pair + 1)


def head(waveform, valid_count, me, parts):
    rows, segs, samples = waveform.shape
    basis = jnp.asarray(make_basis(samples, parts), dtype=jnp.bfloat16)
    vmem = pl.BlockSpec(memory_space=pltpu.VMEM)
    pairs = parts // 2
    block = (2, F // parts, segs, rows)
    return pl.pallas_call(
        functools.partial(head_kernel, parts=parts),
        out_shape=[jax.ShapeDtypeStruct((n,) + block, jnp.bfloat16) for n in [1] * pairs + [pairs]],
        in_specs=[pl.BlockSpec(memory_space=pltpu.SMEM), pl.BlockSpec(memory_space=pltpu.HBM), vmem, vmem],
        out_specs=[vmem] * (pairs + 1),
        scratch_shapes=[
            pltpu.VMEM(waveform.shape, waveform.dtype),
            pltpu.VMEM((segs, rows, samples), jnp.bfloat16),
            pltpu.VMEM((segs, 2 * F, rows), jnp.float32),
            pltpu.SemaphoreType.DMA((8,)),
        ],
        compiler_params=pltpu.CompilerParams(vmem_limit_bytes=48 * MIB),
        name="spectra",
    )(me[None].astype(jnp.int32), waveform, valid_count.T, basis)


def cross_kernel(select_ref, *rest, groups, held, low):
    pieces = len(held)
    sides = [rest[e * pieces : (e + 1) * pieces] for e in range(groups)]
    out_ref, held_ref, sems = rest[-3:]
    side_shape = sides[0][0].shape
    rows, columns = side_shape[-1], side_shape[-1]
    rounds, tiles_across = out_ref.shape[2] // (rows * (columns // LANES)), columns // LANES
    chunk = select_ref.shape[0] // rounds
    step, last = pl.program_id(0), pl.num_programs(0) - 1
    slot = step % 2
    k = low + step
    tiles = [(part, first) for part in range(2) for first in range(0, rows, chunk)]

    def copy(n, slot, k):
        part, first = tiles[n]
        height = rounds * tiles_across
        block = pl.ds(first * height, chunk * height)
        return pltpu.make_async_copy(held_ref.at[slot, part, block], out_ref.at[k, part, block], sems.at[slot, n])

    def whole(e, part):
        return jnp.concatenate(
            [ref[:, part, k - first].reshape(-1, columns) for first, ref in zip(held, sides[e])], axis=0
        )

    real, imag = whole(0, 0), whole(0, 1)
    seg_total = real.shape[0]
    real, imag = real.T, imag.T
    left = jnp.concatenate(
        [jnp.concatenate([real, imag], axis=1), jnp.concatenate([imag, -real], axis=1)], axis=0
    )
    sums = []
    for e in range(groups):
        right = jnp.concatenate([whole(e, 0), whole(e, 1)], axis=0)
        total = jnp.dot(left, right, preferred_element_type=jnp.float32) / float(seg_total)
        sums.append(total.astype(jnp.bfloat16))

    @pl.when(step >= 2)
    def _():
        for n in range(len(tiles)):
            copy(n, slot, k - 2).wait()

    for n, (part, first) in enumerate(tiles):
        start = part * rows + first
        values = jnp.concatenate([total[start : start + chunk] for total in sums], axis=0)
        filled = jnp.dot(select_ref[...], values, preferred_element_type=jnp.float32)
        filled = filled.reshape(chunk, rounds, columns)
        filled = jnp.stack([filled[:, :, q * LANES : (q + 1) * LANES] for q in range(tiles_across)], axis=1)
        height = rounds * tiles_across
        held_ref[slot, part, first * height : (first + chunk) * height] = filled.reshape(
            chunk * height, LANES
        ).astype(jnp.bfloat16)
        copy(n, slot, k).start()

    @pl.when(step == last)
    def _():
        for n in range(len(tiles)):
            copy(n, slot, k).wait()

    @pl.when((step == last) & (step > 0))
    def _():
        for n in range(len(tiles)):
            copy(n, 1 - slot, k - 1).wait()


def selection(offset, groups, rows):
    chunk = max(16, rows // groups)
    shape = (chunk, offset.shape[0], groups, chunk)
    pick = lax.broadcasted_iota(jnp.int32, shape, 2) == offset[None, :, None, None]
    same = lax.broadcasted_iota(jnp.int32, shape, 0) == lax.broadcasted_iota(jnp.int32, shape, 3)
    return (pick & same).astype(jnp.bfloat16).reshape(chunk * offset.shape[0], groups * chunk)


def add_bins(out, select, sides, held, low, high, bins_local, rounds):
    groups = len(sides)
    segs, rows = sides[0][0].shape[3:]
    seg_total = segs * sum(piece.shape[0] for piece in sides[0])
    pieces = [piece for side in sides for piece in side]
    bins = high - low
    aliased = out is not None
    vmem = pl.BlockSpec(memory_space=pltpu.VMEM)
    return pl.pallas_call(
        functools.partial(cross_kernel, groups=groups, held=held, low=low),
        grid=(bins,),
        out_shape=jax.ShapeDtypeStruct((bins_local, 2, rows * rounds * (rows // LANES), LANES), jnp.bfloat16),
        in_specs=[vmem] * (1 + len(pieces)) + [pl.BlockSpec(memory_space=pltpu.HBM)] * aliased,
        out_specs=pl.BlockSpec(memory_space=pltpu.HBM),
        scratch_shapes=[
            pltpu.VMEM((2, 2, rows * rounds * (rows // LANES), LANES), jnp.bfloat16),
            pltpu.SemaphoreType.DMA((2, 2 * rows * rounds // select.shape[0])),
        ],
        input_output_aliases={1 + len(pieces): 0} if aliased else {},
        compiler_params=pltpu.CompilerParams(vmem_limit_bytes=40 * MIB),
        cost_estimate=pl.CostEstimate(
            flops=8 * bins * groups * rows * rows * seg_total,
            bytes_accessed=4 * bins * rows * rounds * rows,
            transcendentals=0,
        ),
        name="cross",
    )(select, *pieces, *([out] if aliased else []))


class Lane:
    def __init__(self, window):
        self.window = window
        self.sent = []

    def send(self, block, axis, pairs, after=()):
        after = list(after) + self.sent[-self.window :][: len(self.sent) // self.window and 1]
        if after:
            block, _ = lax.optimization_barrier((block, after))
        self.sent.append(lax.ppermute(block, axis, pairs))
        return self.sent[-1]


def shards(waveform, valid_count, plan):
    groups = lax.axis_size("grp")
    parts = lax.axis_size("seg")
    chips = parts // PLANES // 2
    bins_local = F // parts
    middle = (4 * bins_local + 4) // 8
    group = lax.axis_index("grp")
    rounds = plan.shape[1]
    offset = lax.dynamic_index_in_dim(plan, group, 0, keepdims=False) ^ group
    select = selection(offset, groups, waveform.shape[0])

    *mine, for_sibling = head(waveform, valid_count, lax.axis_index("seg"), parts)
    theirs = lax.ppermute(for_sibling, "seg", [(s, s ^ 1) for s in range(parts)])
    seg_lane, far_lane, grp_lane = Lane(parts), Lane(2), Lane(3 * (groups - 1))
    sides = [[] for _ in range(groups)]

    def both(n, low=0, high=bins_local):
        return jnp.concatenate([mine[n], theirs[n : n + 1]], axis=0)[:, :, low:high]

    def scatter(lane, n, low=0, high=bins_local, after=()):
        return lane.send(both(n, low, high), "seg", [(s, s ^ (2 * n)) for s in range(parts)], after)

    def forward(blocks):
        block = jnp.concatenate(blocks, axis=0) if len(blocks) > 1 else blocks[0]
        sides[0].append(block)
        for e in range(1, groups):
            sides[e].append(grp_lane.send(block, "grp", [(g, g ^ e) for g in range(groups)]))
        return sides[1][-1]

    own, beside, far, farthest = (range(p * chips, (p + 1) * chips) for p in range(PLANES))
    forward([both(own[0])])
    own_blocks = [scatter(seg_lane, n) for n in own[1:]]
    own_blocks, select = lax.optimization_barrier((own_blocks, select))
    own_done = forward(own_blocks)
    far_blocks = [scatter(far_lane, n, after=own_blocks if n > far[0] else ()) for n in far]
    beside_blocks = [scatter(seg_lane, n, after=far_blocks[:1] if n > beside[0] else ()) for n in beside]
    beside_done = [forward([block]) for block in beside_blocks][-1]
    far_done = [forward([block]) for block in far_blocks]
    waits = {farthest[0]: [own_done], farthest[-1]: [beside_done]}
    *most, last = [scatter(far_lane, n, after=waits.get(n, ())) for n in farthest]
    for block in most:
        forward([block])
    whole = len(sides[0])
    parts_of_bins = ((0, middle), (middle, bins_local))
    for low, high in parts_of_bins:
        forward([last[:, :, low:high]])

    out = None
    for n, (low, high) in enumerate(parts_of_bins):
        chosen = [side[:whole] + side[whole + n :][:1] for side in sides]
        out = add_bins(out, select, chosen, [0] * whole + [low], low, high, bins_local, rounds)
    rows = waveform.shape[0]
    out = out.reshape(bins_local, 2, rows, rows // LANES, rounds, LANES).transpose(0, 1, 2, 4, 3, 5)
    return out.reshape(bins_local, 2, rows, rounds, rows)


def solution(mesh):
    return jax.shard_map(
        shards,
        mesh=mesh,
        in_specs=(P("grp", "seg", None), P("grp", "seg"), P()),
        out_specs=P("seg", None, "grp", None, None),
        check_vma=False,
    )
```

```python
import functools
import math

import jax
import jax.numpy as jnp
from jax import lax
from jax.experimental import pallas as pl
from jax.experimental.pallas import tpu as pltpu
from jax.sharding import PartitionSpec as P

F = 128
LANES = 128
K0 = 2
PLANES = 4
MIB = 1024 * 1024


def fill_basis(basis_ref, parts):
    rows, samples = basis_ref.shape
    bins_local = F // parts
    row = lax.broadcasted_iota(jnp.int32, (rows, LANES), 0)
    lane = lax.broadcasted_iota(jnp.int32, (rows, LANES), 1)
    part = row // bins_local % 2
    bins = K0 + row // (2 * bins_local) * bins_local + row % bins_local
    for q in range(samples // LANES):
        turn = ((lane + q * LANES) * bins + part * (samples // 4)) % samples
        x = (samples // 4 - jnp.minimum(turn, samples - turn)).astype(jnp.float32) * (2.0 * math.pi / samples)
        x2 = x * x
        series = 1.0 / 362880 - x2 * (1.0 / 39916800)
        for term in (-1.0 / 5040, 1.0 / 120, -1.0 / 6, 1.0):
            series = term + x2 * series
        basis_ref[:, q * LANES : (q + 1) * LANES] = (x * series).astype(jnp.bfloat16)


def swap_matrix(outer, inner):
    shape = (inner * outer, inner * outer)
    row, column = (lax.broadcasted_iota(jnp.int32, shape, axis) for axis in range(2))
    source = (row % outer) * inner + row // outer
    return (source == column).astype(jnp.float32).astype(jnp.bfloat16)


def head_kernel(me_ref, wave_ref, valid_ref, *rest, parts):
    out_refs, (held_ref, gated_ref, white_ref, basis_ref, sems) = rest[:-5], rest[-5:]
    rows, segs, samples = wave_ref.shape
    half = samples // 2
    step, copies = 16, sems.shape[0]
    share = rows // copies

    def copy(n):
        part = pl.ds(n * share, share)
        return pltpu.make_async_copy(wave_ref.at[part], held_ref.at[part], sems.at[n])

    for n in range(copies):
        copy(n).start()
    fill_basis(basis_ref, parts)
    valid_rows = valid_ref[...]
    valid_cols = valid_rows.T
    times = lax.broadcasted_iota(jnp.int32, (step * segs, samples), 1)
    to_segs = swap_matrix(step, segs)
    for first in range(0, rows, step):
        if first % share == 0:
            copy(first // share).wait()
        block = held_ref[first : first + step].reshape(step * segs, samples)
        block = jnp.dot(to_segs, block, preferred_element_type=jnp.float32)
        count = jnp.concatenate([valid_cols[first : first + step, s : s + 1] for s in range(segs)], axis=0)
        block = jnp.where(times < count, block, 0.0).astype(jnp.bfloat16)
        gated_ref[:, first : first + step] = block.reshape(segs, step, samples)

    for s in range(segs):
        spectrum = lax.dot_general(
            basis_ref[...], gated_ref[s], (((1,), (1,)), ((), ())), preferred_element_type=jnp.float32
        )
        power = jnp.sum(spectrum * spectrum, axis=0, keepdims=True) / F
        keep = (valid_rows[s : s + 1, :] >= half).astype(jnp.float32)
        white_ref[s] = spectrum * (keep / jnp.sqrt(power + 1e-06))

    me = me_ref[0]
    span = 2 * F // parts
    to_bins = swap_matrix(segs, span)

    def block_for(d):
        first = pl.multiple_of((me ^ d) * span, span)
        piece = jnp.concatenate([white_ref[s, pl.ds(first, span), :] for s in range(segs)], axis=0)
        piece = jnp.dot(to_bins, piece.astype(jnp.bfloat16), preferred_element_type=jnp.float32)
        return piece.astype(jnp.bfloat16).reshape(2, span // 2, segs, rows)

    for pair, out_ref in enumerate(out_refs[:-1]):
        out_ref[0] = block_for(2 * pair)
        out_refs[-1][pair] = block_for(2 * pair + 1)


def head(waveform, valid_count, me, parts):
    rows, segs, samples = waveform.shape
    vmem = pl.BlockSpec(memory_space=pltpu.VMEM)
    pairs = parts // 2
    block = (2, F // parts, segs, rows)
    return pl.pallas_call(
        functools.partial(head_kernel, parts=parts),
        out_shape=[jax.ShapeDtypeStruct((n,) + block, jnp.bfloat16) for n in [1] * pairs + [pairs]],
        in_specs=[pl.BlockSpec(memory_space=pltpu.SMEM), pl.BlockSpec(memory_space=pltpu.HBM), vmem],
        out_specs=[vmem] * (pairs + 1),
        scratch_shapes=[
            pltpu.VMEM(waveform.shape, waveform.dtype),
            pltpu.VMEM((segs, rows, samples), jnp.bfloat16),
            pltpu.VMEM((segs, 2 * F, rows), jnp.float32),
            pltpu.VMEM((2 * F, samples), jnp.bfloat16),
            pltpu.SemaphoreType.DMA((8,)),
        ],
        compiler_params=pltpu.CompilerParams(vmem_limit_bytes=48 * MIB),
        name="spectra",
    )(me[None].astype(jnp.int32), waveform, valid_count.T)


def cross_kernel(select_ref, *rest, groups, held, low):
    pieces = len(held)
    sides = [rest[e * pieces : (e + 1) * pieces] for e in range(groups)]
    out_ref, held_ref, sems = rest[-3:]
    side_shape = sides[0][0].shape
    rows, columns = side_shape[-1], side_shape[-1]
    rounds, tiles_across = out_ref.shape[2] // (rows * (columns // LANES)), columns // LANES
    chunk = select_ref.shape[0] // rounds
    step, last = pl.program_id(0), pl.num_programs(0) - 1
    slot = step % 2
    k = low + step
    tiles = [(part, first) for part in range(2) for first in range(0, rows, chunk)]

    def copy(n, slot, k):
        part, first = tiles[n]
        height = rounds * tiles_across
        block = pl.ds(first * height, chunk * height)
        return pltpu.make_async_copy(held_ref.at[slot, part, block], out_ref.at[k, part, block], sems.at[slot, n])

    def whole(e, part):
        return jnp.concatenate(
            [ref[:, part, k - first].reshape(-1, columns) for first, ref in zip(held, sides[e])], axis=0
        )

    real, imag = whole(0, 0), whole(0, 1)
    seg_total = real.shape[0]
    real, imag = real.T, imag.T
    left = jnp.concatenate(
        [jnp.concatenate([real, imag], axis=1), jnp.concatenate([imag, -real], axis=1)], axis=0
    )
    sums = []
    for e in range(groups):
        right = jnp.concatenate([whole(e, 0), whole(e, 1)], axis=0)
        total = jnp.dot(left, right, preferred_element_type=jnp.float32) / float(seg_total)
        sums.append(total.astype(jnp.bfloat16))

    @pl.when(step >= 2)
    def _():
        for n in range(len(tiles)):
            copy(n, slot, k - 2).wait()

    for n, (part, first) in enumerate(tiles):
        start = part * rows + first
        values = jnp.concatenate([total[start : start + chunk] for total in sums], axis=0)
        filled = jnp.dot(select_ref[...], values, preferred_element_type=jnp.float32)
        filled = filled.reshape(chunk, rounds, columns)
        filled = jnp.stack([filled[:, :, q * LANES : (q + 1) * LANES] for q in range(tiles_across)], axis=1)
        height = rounds * tiles_across
        held_ref[slot, part, first * height : (first + chunk) * height] = filled.reshape(
            chunk * height, LANES
        ).astype(jnp.bfloat16)
        copy(n, slot, k).start()

    @pl.when(step == last)
    def _():
        for n in range(len(tiles)):
            copy(n, slot, k).wait()

    @pl.when((step == last) & (step > 0))
    def _():
        for n in range(len(tiles)):
            copy(n, 1 - slot, k - 1).wait()


def selection(offset, groups, rows):
    chunk = max(16, rows // groups)
    shape = (chunk, offset.shape[0], groups, chunk)
    pick = lax.broadcasted_iota(jnp.int32, shape, 2) == offset[None, :, None, None]
    same = lax.broadcasted_iota(jnp.int32, shape, 0) == lax.broadcasted_iota(jnp.int32, shape, 3)
    return (pick & same).astype(jnp.bfloat16).reshape(chunk * offset.shape[0], groups * chunk)


def add_bins(out, select, sides, held, low, high, bins_local, rounds):
    groups = len(sides)
    segs, rows = sides[0][0].shape[3:]
    seg_total = segs * sum(piece.shape[0] for piece in sides[0])
    pieces = [piece for side in sides for piece in side]
    bins = high - low
    aliased = out is not None
    vmem = pl.BlockSpec(memory_space=pltpu.VMEM)
    return pl.pallas_call(
        functools.partial(cross_kernel, groups=groups, held=held, low=low),
        grid=(bins,),
        out_shape=jax.ShapeDtypeStruct((bins_local, 2, rows * rounds * (rows // LANES), LANES), jnp.bfloat16),
        in_specs=[vmem] * (1 + len(pieces)) + [pl.BlockSpec(memory_space=pltpu.HBM)] * aliased,
        out_specs=pl.BlockSpec(memory_space=pltpu.HBM),
        scratch_shapes=[
            pltpu.VMEM((2, 2, rows * rounds * (rows // LANES), LANES), jnp.bfloat16),
            pltpu.SemaphoreType.DMA((2, 2 * rows * rounds // select.shape[0])),
        ],
        input_output_aliases={1 + len(pieces): 0} if aliased else {},
        compiler_params=pltpu.CompilerParams(vmem_limit_bytes=40 * MIB),
        cost_estimate=pl.CostEstimate(
            flops=8 * bins * groups * rows * rows * seg_total,
            bytes_accessed=4 * bins * rows * rounds * rows,
            transcendentals=0,
        ),
        name="cross",
    )(select, *pieces, *([out] if aliased else []))


class Lane:
    def __init__(self, window):
        self.window = window
        self.sent = []

    def send(self, block, axis, pairs, after=()):
        after = list(after) + self.sent[-self.window :][: len(self.sent) // self.window and 1]
        if after:
            block, _ = lax.optimization_barrier((block, after))
        self.sent.append(lax.ppermute(block, axis, pairs))
        return self.sent[-1]


def shards(waveform, valid_count, plan):
    groups = lax.axis_size("grp")
    parts = lax.axis_size("seg")
    chips = parts // PLANES // 2
    bins_local = F // parts
    middle = (5 * bins_local + 4) // 8
    group = lax.axis_index("grp")
    rounds = plan.shape[1]
    offset = lax.dynamic_index_in_dim(plan, group, 0, keepdims=False) ^ group
    select = selection(offset, groups, waveform.shape[0])

    *mine, for_sibling = head(waveform, valid_count, lax.axis_index("seg"), parts)
    theirs = lax.ppermute(for_sibling, "seg", [(s, s ^ 1) for s in range(parts)])
    seg_lane, far_lane, grp_lane = Lane(parts), Lane(2), Lane(2 * (groups - 1))
    sides = [[] for _ in range(groups)]

    def both(n, low=0, high=bins_local):
        return jnp.concatenate([mine[n], theirs[n : n + 1]], axis=0)[:, :, low:high]

    def scatter(lane, n, low=0, high=bins_local, after=()):
        return lane.send(both(n, low, high), "seg", [(s, s ^ (2 * n)) for s in range(parts)], after)

    def forward(blocks):
        block = jnp.concatenate(blocks, axis=0) if len(blocks) > 1 else blocks[0]
        sides[0].append(block)
        for e in range(1, groups):
            sides[e].append(grp_lane.send(block, "grp", [(g, g ^ e) for g in range(groups)]))
        return sides[1][-1]

    own, beside, far, farthest = (range(p * chips, (p + 1) * chips) for p in range(PLANES))
    forward([both(own[0])])
    own_blocks = [scatter(seg_lane, n) for n in own[1:]]
    own_blocks, select = lax.optimization_barrier((own_blocks, select))
    own_done = forward(own_blocks)
    waits = {(0, n): own_blocks for n in far[1:]}
    first = [scatter(far_lane, n, 0, middle, waits.get((0, n), ())) for n in far]
    beside_blocks = [scatter(seg_lane, n, after=first[:1] if n > beside[0] else ()) for n in beside]
    beside_done = [forward([block]) for block in beside_blocks]
    far_done = forward(first)
    first = [scatter(far_lane, n, 0, middle, beside_done[:1] if n == farthest[-1] else ()) for n in farthest]
    last_done = [forward([block]) for block in first]
    second = [scatter(far_lane, far[0], middle, bins_local, beside_done[-1:])]
    second += [scatter(far_lane, n, middle, bins_local, [far_done]) for n in far[1:]]
    forward(second)
    split = 1 + chips
    whole = len(sides[0]) - 1 - split
    out = add_bins(
        None, select, [side[: whole + split] for side in sides], [0] * (whole + split), 0, middle, bins_local, rounds
    )
    second = [scatter(far_lane, n, middle, bins_local, last_done[:1]) for n in farthest]
    second[0], out = lax.optimization_barrier((second[0], out))
    for block in second:
        forward([block])
    chosen = [side[:whole] + side[-split:] for side in sides]
    out = add_bins(out, select, chosen, [0] * whole + [middle] * split, middle, bins_local, bins_local, rounds)
    rows = waveform.shape[0]
    out = out.reshape(bins_local, 2, rows, rows // LANES, rounds, LANES).transpose(0, 1, 2, 4, 3, 5)
    return out.reshape(bins_local, 2, rows, rounds, rows)


def solution(mesh):
    return jax.shard_map(
        shards,
        mesh=mesh,
        in_specs=(P("grp", "seg", None), P("grp", "seg"), P()),
        out_specs=P("seg", None, "grp", None, None),
        check_vma=False,
    )
```
